768 devices in a mesh: outer: 16 (over z_hi, x, core), inner: 48 (over y, z_lo).
Axes of the slice: x: 4, y: 8, z: 12 (z_hi: 2, z_lo: 6; z = z_hi * 6 + z_lo), core: 2. Of those that a mesh axis runs over, the one named last changes fastest.
Arguments:
- acts: bfloat16 [4096, 12288], P('outer', 'inner'), may hold values from -6 to 6
- codes: bfloat16 [12288, 6144], P('inner', 'outer'), may hold values from -1.6953125 to 1.6953125
- scales: float32 [48, 12288], P('outer', 'inner'), may hold values from 0.0027063293 to 0.027063293
- routes: int32 [4096, 2], P('outer'), may hold values from 0 to 7, as said below
- route_logits: float32 [4096, 2], P('outer'), may hold values from -6 to 6
- cotangent: bfloat16 [4096, 6144], P('outer'), may hold values from -6 to 6
Outputs:
- mixed: bfloat16 [4096, 6144], P('outer', 'inner')
- act_grad: bfloat16 [4096, 12288], P('outer', 'inner')
- weight_grad: float32 [12288, 6144], P('inner', 'outer')
The draws below stay inside these ranges and needn't reach their ends.
Inputs may be any that keep to these rules, and one draw needn't show every extreme that they name: `routes`: each token names expert 0 exactly once and one other expert.
All inputs are finite; a program needn't handle non-finite values.
Results may differ from the reference program's by a relative error of at most 0.015.
Values may be sent and summed in bfloat16 or wider, within the bound.
A program may use at most 64 MiB of HBM per device.

```python
import math
import jax
import jax.numpy as jnp
from jax import lax

D = 6144
BLOCK = 128
TOK_DEV = 256
FF = 12288
TOKENS = 4096
N_OUTER = 16


def draw_routes(key, part):
    key = jax.random.fold_in(key, 11)
    order_key, slot_key = jax.random.split(key)
    shuffled = jax.random.permutation(order_key, TOKENS).astype(jnp.int32)
    second = (1 + shuffled % 7).astype(jnp.int32)
    slot = jax.random.randint(slot_key, (TOKENS,), 0, 2).astype(jnp.int32)
    first_col = jnp.where(slot == 0, jnp.zeros_like(second), second)
    second_col = jnp.where(slot == 0, second, jnp.zeros_like(second))
    return jnp.stack([first_col, second_col], axis=1).astype(jnp.int32)


def block_scale(key, extent, pieces, low, largest):
    gain, own = 1.0, jax.random.fold_in(key, 6)
    for axis_at, parts in pieces:
        draws = jnp.exp(jax.random.uniform(jax.random.fold_in(own, axis_at), (parts,), jnp.float32, low / len(pieces), largest / len(pieces)))
        gain = gain * jnp.repeat(draws, extent[axis_at] // parts).reshape([-1 if axis == axis_at else 1 for axis in range(len(extent))])
    return gain


def centred(rng, shape, scale, most, pieces=(), dtype=jnp.bfloat16):
    result = jax.random.normal(rng, shape, jnp.float32) * scale
    if len(pieces) > 0:
        result = block_scale(rng, shape, pieces, -0.22, 0.18) * result
    return jnp.clip(result, min=-most, max=most).astype(dtype)


def setup_inputs(seed: int = 0) -> dict:
    splits = jax.random.split(jax.random.key(seed), 7)
    acts = centred(splits[0], (TOKENS, FF), 1.0, 6.0, ((0, 16), (1, 48)))
    codes = jnp.clip(jax.random.uniform(splits[1], (FF, D), jnp.float32, -1.6953125, 1.6953125) * block_scale(splits[1], (FF, D), ((0, 48), (1, 16)), -0.4, 0.0), -1.6953125, 1.6953125).astype(jnp.bfloat16)
    scales = jnp.clip(jnp.exp(math.log(0.027063293) - 2.3025851 * jax.random.uniform(splits[2], (D // BLOCK, FF), jnp.float32) ** block_scale(splits[2], (D // BLOCK, FF), ((0, 16), (1, 48)), -0.2, 0.2)), 0.0027063293, 0.027063293)
    routes = draw_routes(jax.random.fold_in(splits[6], 71), 0)
    route_logits = centred(splits[4], (TOKENS, 2), 1.5, 6.0, ((0, 16),), jnp.float32)
    cotangent = centred(splits[5], (TOKENS, D), 1.0, 6.0, ((0, 16),))
    return {"acts": acts, "codes": codes, "scales": scales, "routes": routes, "route_logits": route_logits, "cotangent": cotangent}


def reference(acts, codes, scales, routes, route_logits, cotangent):
    expanded = jnp.repeat(scales.T, BLOCK, axis=1)
    weight = (codes.astype(jnp.float32) * expanded).astype(jnp.bfloat16)
    probs = jax.nn.softmax(route_logits.astype(jnp.float32), axis=-1)
    coef = jnp.sum(probs * (routes == 0).astype(jnp.float32), axis=-1)
    mixed = (coef[:, None] * jnp.dot(acts, weight, preferred_element_type=jnp.float32)).astype(jnp.bfloat16)
    scaled = (coef[:, None] * cotangent.astype(jnp.float32)).astype(jnp.bfloat16)
    act_grad = jnp.dot(scaled, weight.T, preferred_element_type=jnp.float32).astype(jnp.bfloat16)
    groups_a = acts.reshape(N_OUTER, TOK_DEV, FF)
    groups_g = scaled.reshape(N_OUTER, TOK_DEV, D)

    def add_group(total, pair):
        part = jnp.dot(pair[0].T, pair[1], preferred_element_type=jnp.float32).astype(jnp.bfloat16)
        part = lax.optimization_barrier(part)
        return total + part.astype(jnp.float32), None

    weight_grad, unused = lax.scan(add_group, jnp.zeros((FF, D), jnp.float32), (groups_a, groups_g))
    return mixed, act_grad, weight_grad
```

```python
import jax
import jax.numpy as jnp
from jax import lax
from jax.experimental import pallas as pl
from jax.experimental.pallas import tpu as pltpu
from jax.sharding import PartitionSpec as P

MESH = pl.DeviceIdType.MESH
BF16 = jnp.bfloat16
F32 = jnp.float32
NX, NY, NZ, NO = 4, 8, 6, 16
TOK, FFD, COLS = 256, 256, 384
HALF = FFD // 2
N_A, N_B, N_C = 24, 6, 14


def kernel(
    acts_ref, codes_ref, scales_ref, routes_ref, logits_ref, cot_ref,
    mixed_ref, act_grad_ref, wgrad_ref,
    weight, scaled, coef, acts_t, term_out, term_in, term,
    x1_out, x1_in, x2_out, x2_in, z_out, z_in,
    y_out, y_in, m_own, m_out, m_in, acc,
    a_send, a_recv, b_send, b_recv, c_send, c_recv, m_send, m_recv,
):
    o = lax.axis_index("outer")
    i = lax.axis_index("inner")
    core = lax.rem(o, 2)
    x = lax.rem(lax.div(o, 2), NX)
    hi = lax.div(o, 2 * NX)
    y = lax.div(i, NZ)
    z = lax.rem(i, NZ)

    def out_index(hi_, x_, core_):
        return (hi_ * NX + x_) * 2 + core_

    def xp(n):
        return lax.rem(x + n + NX, NX)

    def yp(n):
        return lax.rem(y + n + NY, NY)

    sibling = (out_index(hi, x, 1 - core), i)
    partner = (out_index(1 - hi, x, core), i)
    right, left = (out_index(hi, xp(1), core), i), (out_index(hi, xp(-1), core), i)
    up, down = (o, yp(1) * NZ + z), (o, yp(-1) * NZ + z)

    barrier = pltpu.get_barrier_semaphore()
    for peer in (sibling, partner, right, left, up, down):
        pl.semaphore_signal(barrier, inc=1, device_id=peer, device_id_type=MESH)
    for n in range(1, NZ):
        pl.semaphore_signal(barrier, inc=1, device_id=(o, y * NZ + lax.rem(z + n, NZ)), device_id_type=MESH)

    for b in range(3):
        cols = pl.ds(b * 128, 128)
        weight[o, :, cols] = (codes_ref[:, cols].astype(F32) * scales_ref[:, b : b + 1]).astype(BF16)
    pl.semaphore_wait(barrier, 6 + NZ - 1)

    sent = []

    def send(src, dst, ssem, rsem, peer):
        copy = pltpu.make_async_remote_copy(
            src_ref=src, dst_ref=dst, send_sem=ssem, recv_sem=rsem, device_id=peer, device_id_type=MESH
        )
        copy.start()
        sent.append(copy)
        return copy

    def block(slot, half):
        return weight.at[slot, pl.ds(half * HALF, HALF)]

    def send_a(n, slot, half, peer):
        ref = block(slot, half)
        return send(ref, ref, a_send.at[n], a_recv.at[n], peer)

    a_z = [send_a(h, o, h, partner) for h in range(2)]
    a_r = [[send_a(2 + h, o, h, right) for h in range(2)], None]
    a_l = [[send_a(4 + h, o, h, left) for h in range(2)], None]

    def share(n, slot):
        ref = weight.at[slot]
        return send(ref, ref, a_send.at[16 + n], a_recv.at[16 + n], sibling)

    a_s = [share(0, o)]

    lg = logits_ref[...]
    top = jnp.max(lg, axis=-1, keepdims=True)
    ex = jnp.exp(lg - top)
    probs = ex / jnp.sum(ex, axis=-1, keepdims=True)
    coef[...] = jnp.sum(probs * (routes_ref[...] == 0).astype(F32), axis=-1, keepdims=True)
    acts_t[...] = acts_ref[...].T

    def scale_block(n, carry):
        cols = pl.ds(pl.multiple_of(n * COLS, 128), COLS)
        scaled[n] = (coef[...] * cot_ref[:, cols].astype(F32)).astype(BF16)
        return carry

    lax.fori_loop(0, NO, scale_block, 0)

    def term_other(n, carry):
        term_out[n] = jnp.dot(acts_t[...], scaled[2 * n + 1 - core], preferred_element_type=F32).astype(BF16)
        return carry

    lax.fori_loop(0, 8, term_other, 0)
    b_pair = send(term_out, term_in, b_send.at[0], b_recv.at[0], sibling)

    def forward(stage, hi_):
        base = (6, 14)[stage]
        got_r, got_l = a_r[stage], a_l[stage]
        got_r[0].wait_recv()
        f_r = send_a(base, out_index(hi_, xp(-1), core), 0, right)
        got_l[1].wait_recv()
        f_l = send_a(base + 1, out_index(hi_, xp(1), core), 1, left)
        got_r[1].wait_recv()
        a_s.append(share(1 + 4 * stage, out_index(hi_, xp(-1), core)))
        got_l[0].wait_recv()
        a_s.append(share(2 + 4 * stage, out_index(hi_, xp(1), core)))
        return f_r, f_l

    def finish(stage, hi_, f_r, f_l):
        f_r.wait_recv()
        f_l.wait_recv()
        a_s.append(share(3 + 4 * stage, out_index(hi_, xp(2), core)))

    f_own = forward(0, hi)

    def term_own(n, carry):
        term[n] = jnp.dot(acts_t[...], scaled[2 * n + core], preferred_element_type=F32).astype(BF16)
        return carry

    lax.fori_loop(0, 8, term_own, 0)

    finish(0, hi, *f_own)
    p_slot = out_index(1 - hi, x, core)
    a_r[1], a_l[1] = [], []
    for h in range(2):
        a_z[h].wait_recv()
        a_r[1].append(send_a(8 + h, p_slot, h, right))
        a_l[1].append(send_a(12 + h, p_slot, h, left))
    a_s.append(share(4, p_slot))
    f_far = forward(1, 1 - hi)

    b_pair.wait_recv()

    def far_half(w, half):
        rows = pl.ds(half * HALF, HALF)
        n = w * NX + xp(2)
        return (term[n, rows].astype(F32) + term_in[n, rows].astype(F32)).astype(BF16)

    for w in range(2):
        for d in range(2):
            x1_out[d, w] = far_half(w, d)
    b_x1 = [send(x1_out.at[d], x1_in.at[d], b_send.at[1 + d], b_recv.at[1 + d], (right, left)[d]) for d in range(2)]

    finish(1, 1 - hi, *f_far)
    for copy in a_s:
        copy.wait_recv()

    def product(dest, piece):
        return jnp.dot(acts_ref[...], weight[2 * dest + piece], preferred_element_type=F32)

    def send_c(n, dest, piece, peer, prior):
        value = product(dest, piece)
        if prior is not None:
            k, copy = prior
            copy.wait_recv()
            value = value + y_in[k].astype(F32)
        y_out[n] = value.astype(BF16)
        return n, send(y_out.at[n], y_in.at[n], c_send.at[n], c_recv.at[n], peer)

    up0 = send_c(0, yp(4), 0, up, None)
    dn1 = send_c(7, yp(-4), 1, down, None)
    up1 = send_c(1, yp(3), 1, up, None)
    dn0 = send_c(8, yp(-3), 0, down, None)

    acc[...] = jnp.zeros_like(acc)

    def grad_block(n, carry):
        acc[...] += lax.dot_general(
            scaled[n], weight[n], (((1,), (1,)), ((), ())), preferred_element_type=F32
        )
        return carry

    lax.fori_loop(0, NO, grad_block, 0)
    act_grad_ref[...] = acc[...].astype(BF16)

    up0 = send_c(2, yp(3), 0, up, up0)
    dn1 = send_c(9, yp(-3), 1, down, dn1)

    for d in range(2):
        b_x1[d].wait_recv()
    for d in range(2):
        near = xp(1 - 2 * d)
        other = pl.ds((1 - d) * HALF, HALF)
        rows = pl.ds(d * HALF, HALF)
        for w in range(2):
            n = w * NX + near
            x2_out[d, w, other] = (term[n, other].astype(F32) + term_in[n, other].astype(F32)).astype(BF16)
            x2_out[d, w, rows] = (
                term[n, rows].astype(F32) + term_in[n, rows].astype(F32) + x1_in[d, w].astype(F32)
            ).astype(BF16)
    b_x2 = [send(x2_out.at[d], x2_in.at[d], b_send.at[3 + d], b_recv.at[3 + d], (right, left)[d]) for d in range(2)]

    up1 = send_c(3, yp(2), 1, up, up1)
    dn0 = send_c(10, yp(-2), 0, down, dn0)
    up0 = send_c(4, yp(2), 0, up, up0)
    dn1 = send_c(11, yp(-2), 1, down, dn1)

    for d in range(2):
        b_x2[d].wait_recv()

    def reduced(w):
        n = w * NX + x
        return (
            term[n].astype(F32) + term_in[n].astype(F32) + x2_in[0, w].astype(F32) + x2_in[1, w].astype(F32)
        )

    z_out[...] = reduced(1 - hi).astype(BF16)
    b_z = send(z_out, z_in, b_send.at[5], b_recv.at[5], partner)

    up1 = send_c(5, yp(1), 1, up, up1)
    dn0 = send_c(12, yp(-1), 0, down, dn0)
    up0 = send_c(6, yp(1), 0, up, up0)
    dn1 = send_c(13, yp(-1), 1, down, dn1)

    wgrad_ref[...] = reduced(hi)

    for piece in range(2):
        value = product(y, piece)
        for k, copy in ((up0, dn0), (up1, dn1))[piece]:
            copy.wait_recv()
            value = value + y_in[k].astype(F32)
        for b in range(3):
            n = 3 * piece + b
            part = value[:, b * 128 : (b + 1) * 128]
            m_own[n] = part
            m_out[n] = part.astype(BF16)

            @pl.when(z != n)
            def _():
                pltpu.make_async_remote_copy(
                    src_ref=m_out.at[n], dst_ref=m_in.at[z], send_sem=m_send.at[n], recv_sem=m_recv.at[z],
                    device_id=(o, y * NZ + n), device_id_type=MESH,
                ).start()

    b_z.wait_recv()
    wgrad_ref[...] += z_in[...].astype(F32)

    acc[:, :128] = m_own[z]
    for n in range(NZ):

        @pl.when(z != n)
        def _():
            copy = pltpu.make_async_remote_copy(
                src_ref=m_out.at[n], dst_ref=m_in.at[n], send_sem=m_send.at[n], recv_sem=m_recv.at[n],
                device_id=(o, y * NZ + n), device_id_type=MESH,
            )
            copy.wait_recv()
            acc[:, :128] += m_in[n].astype(F32)
            copy.wait_send()

    mixed_ref[...] = (coef[...] * acc[:, :128]).astype(BF16)
    for copy in sent:
        copy.wait_send()


def local(acts, codes, scales, routes, route_logits, cotangent):
    vmem = pl.BlockSpec(memory_space=pltpu.VMEM)
    dma = pltpu.SemaphoreType.DMA
    blk = (FFD, COLS)
    return tuple(
        pl.pallas_call(
            kernel,
            name="expert_down",
            out_shape=(
                jax.ShapeDtypeStruct((TOK, 128), BF16),
                jax.ShapeDtypeStruct((TOK, FFD), BF16),
                jax.ShapeDtypeStruct(blk, F32),
            ),
            in_specs=[vmem] * 6,
            out_specs=[vmem] * 3,
            scratch_shapes=[
                pltpu.VMEM((NO, *blk), BF16),
                pltpu.VMEM((NO, TOK, COLS), BF16),
                pltpu.VMEM((TOK, 1), F32),
                pltpu.VMEM((FFD, TOK), BF16),
                pltpu.VMEM((8, *blk), BF16),
                pltpu.VMEM((8, *blk), BF16),
                pltpu.VMEM((8, *blk), BF16),
                pltpu.VMEM((2, 2, HALF, COLS), BF16),
                pltpu.VMEM((2, 2, HALF, COLS), BF16),
                pltpu.VMEM((2, 2, *blk), BF16),
                pltpu.VMEM((2, 2, *blk), BF16),
                pltpu.VMEM(blk, BF16),
                pltpu.VMEM(blk, BF16),
                pltpu.VMEM((N_C, TOK, COLS), BF16),
                pltpu.VMEM((N_C, TOK, COLS), BF16),
                pltpu.VMEM((NZ, TOK, 128), F32),
                pltpu.VMEM((NZ, TOK, 128), BF16),
                pltpu.VMEM((NZ, TOK, 128), BF16),
                pltpu.VMEM((TOK, FFD), F32),
                dma((N_A,)), dma((N_A,)), dma((N_B,)), dma((N_B,)),
                dma((N_C,)), dma((N_C,)), dma((NZ,)), dma((NZ,)),
            ],
            compiler_params=pltpu.CompilerParams(
                collective_id=0, has_side_effects=True, vmem_limit_bytes=48 * 2**20
            ),
            cost_estimate=pl.CostEstimate(flops=2_500_000_000, bytes_accessed=8_000_000, transcendentals=0),
        )(acts, codes, scales.T, routes, route_logits, cotangent)
    )


def solution(mesh):
    in_specs = (
        P("outer", "inner"),
        P("inner", "outer"),
        P("outer", "inner"),
        P("outer", None),
        P("outer", None),
        P("outer", None),
    )
    out_specs = (P("outer", "inner"), P("outer", "inner"), P("inner", "outer"))
    return jax.shard_map(local, mesh=mesh, in_specs=in_specs, out_specs=out_specs, check_vma=False)
```

```python
import jax
import jax.numpy as jnp
from jax import lax
from jax.experimental import pallas as pl
from jax.experimental.pallas import tpu as pltpu
from jax.sharding import PartitionSpec as P

MESH = pl.DeviceIdType.MESH
BF16 = jnp.bfloat16
F32 = jnp.float32
NX, NY, NZ = 4, 8, 6
TOK, FFD, COLS = 256, 256, 384
HALF = FFD // 2
NS = 3
N_HOP, N_COPY = 14 * NS, 88


def kernel(
    acts_ref, codes_ref, scales_ref, routes_ref, logits_ref, cot_ref,
    mixed_ref, act_grad_ref, wgrad_ref,
    acts_v, codes_v, scales_v, routes_v, logits_v, cot_v,
    weight, scaled, coef, acts_t, term_out, term_in, term,
    x1_out, x1_in, x2_out, x2_in, z_out, z_in,
    prod, y_out, y_in, m_own, m_out, m_in, acc,
    in_sem, s_sem, r_sem, m_send, m_recv,
):
    o = lax.axis_index("outer")
    i = lax.axis_index("inner")
    core = lax.rem(o, 2)
    chip = lax.div(o, 2)
    x = lax.rem(chip, NX)
    hi = lax.div(chip, NX)
    y = lax.div(i, NZ)
    z = lax.rem(i, NZ)

    def xp(n):
        return lax.rem(x + n + NX, NX)

    def yp(n):
        return lax.rem(y + n + NY, NY)

    sibling = (chip * 2 + 1 - core, i)
    partner = (((1 - hi) * NX + x) * 2 + core, i)
    right, left = ((hi * NX + xp(1)) * 2 + core, i), ((hi * NX + xp(-1)) * 2 + core, i)
    up, down = (o, yp(1) * NZ + z), (o, yp(-1) * NZ + z)

    def load(n, src, dst):
        copy = pltpu.make_async_copy(src, dst, in_sem.at[n])
        copy.start()
        return copy

    scales_v[...] = jnp.zeros_like(scales_v)
    loads = [
        load(0, scales_ref, scales_v.at[pl.ds(0, 3)]),
        load(1, codes_ref, codes_v),
        load(2, routes_ref, routes_v),
        load(3, logits_ref, logits_v),
        load(4, acts_ref, acts_v),
        load(5, cot_ref, cot_v),
    ]

    barrier = pltpu.get_barrier_semaphore()
    for peer in (sibling, partner, right, left, up, down):
        pl.semaphore_signal(barrier, inc=1, device_id=peer, device_id_type=MESH)
    for n in range(1, NZ):
        pl.semaphore_signal(barrier, inc=1, device_id=(o, y * NZ + lax.rem(z + n, NZ)), device_id_type=MESH)

    loads[0].wait()
    factors = scales_v[...].T
    loads[1].wait()
    for b in range(NS):
        cols = pl.ds(b * 128, 128)
        weight[chip, core, b] = (codes_v[:, cols].astype(F32) * factors[:, b : b + 1]).astype(BF16)
    pl.semaphore_wait(barrier, 6 + NZ - 1)

    sent = []

    def send(src, dst, peer):
        n = len(sent)
        copy = pltpu.make_async_remote_copy(
            src_ref=src, dst_ref=dst, send_sem=s_sem.at[n], recv_sem=r_sem.at[n],
            device_id=peer, device_id_type=MESH,
        )
        copy.start()
        sent.append(copy)
        return copy

    def same(ref, peer):
        return send(ref, ref, peer)

    far = 1 - hi
    far_z = [same(weight.at[chip, core, b], partner) for b in range(NS)]
    own = weight.at[chip, core]
    own_r, own_l = same(own, right), same(own, left)
    own_shared = [same(own, sibling)]

    loads[2].wait()
    loads[3].wait()
    lg = logits_v[...]
    ex = jnp.exp(lg - jnp.max(lg, axis=0, keepdims=True))
    probs = ex / jnp.sum(ex, axis=0, keepdims=True)
    row = jnp.sum(probs * (routes_v[...] == 0).astype(F32), axis=0, keepdims=True)
    coef[...] = jnp.broadcast_to(row, (8, TOK)).T[:, :1]
    loads[4].wait()
    acts_t[...] = acts_v[...].T
    loads[5].wait()

    def scale_chip(k, carry):
        for c in range(2):
            for b in range(NS):
                cols = pl.ds(pl.multiple_of(k * (2 * COLS), 128) + (c * COLS + b * 128), 128)
                scaled[k, c, b] = (coef[...] * cot_v[:, cols].astype(F32)).astype(BF16)
        return carry

    lax.fori_loop(0, NY, scale_chip, 0)

    def own_near():
        own_r.wait_recv()
        w = weight.at[hi * NX + xp(-1), core]
        f_r = same(w.at[:, pl.ds(0, HALF)], right)
        own_shared.append(same(w, sibling))
        own_l.wait_recv()
        w = weight.at[hi * NX + xp(1), core]
        f_l = same(w.at[:, pl.ds(HALF, HALF)], left)
        own_shared.append(same(w, sibling))
        return f_r, f_l

    own_f = own_near()

    def terms(dst, c):
        def body(k, carry):
            g = jnp.concatenate([scaled[k, c, b] for b in range(NS)], axis=1)
            dst[k] = jnp.dot(acts_t[...], g, preferred_element_type=F32).astype(BF16)
            return carry

        lax.fori_loop(0, NY, body, 0)

    terms(term_out, 1 - core)
    b_pair = send(term_out, term_in, sibling)

    for copy in own_f:
        copy.wait_recv()
    own_shared.append(same(weight.at[hi * NX + xp(2), core], sibling))

    far_x, far_f, far_shared = [None] * NS, [None] * NS, [[] for _ in range(NS)]

    def far_1(b):
        far_z[b].wait_recv()
        w = weight.at[far * NX + x, core, b]
        far_x[b] = same(w, right), same(w, left)
        far_shared[b].append(same(w, sibling))

    def far_2(b):
        far_x[b][0].wait_recv()
        w = weight.at[far * NX + xp(-1), core, b]
        f_r = same(w.at[pl.ds(0, HALF)], right)
        far_shared[b].append(same(w, sibling))
        far_x[b][1].wait_recv()
        w = weight.at[far * NX + xp(1), core, b]
        f_l = same(w.at[pl.ds(HALF, HALF)], left)
        far_shared[b].append(same(w, sibling))
        far_f[b] = f_r, f_l

    def far_3(b):
        for copy in far_f[b]:
            copy.wait_recv()
        far_shared[b].append(same(weight.at[far * NX + xp(2), core, b], sibling))

    def far_4(b):
        if b == 0:
            for copy in own_shared:
                copy.wait_recv()
        for copy in far_shared[b]:
            copy.wait_recv()

    b_x1, b_x2, b_z = [], [], []

    def paired(n, rows):
        return term[n, rows].astype(F32) + term_in[n, rows].astype(F32)

    def half(d):
        return pl.ds(d * HALF, HALF)

    def grad_1():
        b_pair.wait_recv()
        for d in range(2):
            for w in range(2):
                x1_out[d, w] = paired(w * NX + xp(2), half(d)).astype(BF16)
            b_x1.append(send(x1_out.at[d], x1_in.at[d], (right, left)[d]))

    def grad_2():
        for d in range(2):
            for w in range(2):
                n = w * NX + xp(1 - 2 * d)
                x2_out[d, w, half(1 - d)] = paired(n, half(1 - d)).astype(BF16)
        for d in range(2):
            b_x1[d].wait_recv()
            for w in range(2):
                n = w * NX + xp(1 - 2 * d)
                x2_out[d, w, half(d)] = (paired(n, half(d)) + x1_in[d, w].astype(F32)).astype(BF16)
            b_x2.append(send(x2_out.at[d], x2_in.at[d], (right, left)[d]))

    def reduced(w):
        return paired(w * NX + x, pl.ds(0, FFD)) + x2_in[0, w].astype(F32) + x2_in[1, w].astype(F32)

    def grad_3():
        for copy in b_x2:
            copy.wait_recv()
        z_out[...] = reduced(far).astype(BF16)
        b_z.append(send(z_out, z_in, partner))
        wgrad_ref[...] = reduced(hi)

    chains = [{} for _ in range(NS)]

    def product(b, slot, dest):
        w = jnp.concatenate([weight[dest, 0, b], weight[dest, 1, b]], axis=1)
        prod[slot] = jnp.dot(acts_v[...], w, preferred_element_type=F32)

    def hop(b, way, h, slot):
        prior = chains[b].get((way, h))
        value = prod[slot, half(h)]
        if prior is not None:
            n, copy = prior
            copy.wait_recv()
            value = value + y_in[n].astype(F32)
        n = hop.count
        hop.count += 1
        y_out[n] = value.astype(BF16)
        chains[b][(way, h)] = n, send(y_out.at[n], y_in.at[n], (up, down)[way])

    hop.count = 0

    def tick(b, t):
        p_up, p_down = 2 * b, 2 * b + 1
        if t == 0:
            product(b, p_up, yp(4))
            hop(b, 0, 0, p_up)
            hop(b, 1, 1, p_up)
            return
        d = 3 - (t - 1) // 2
        if t == 7:
            product(b, p_up, y)
            for h in range(2):
                value = prod[p_up, half(h)]
                for way in range(2):
                    n, copy = chains[b][(way, h)]
                    copy.wait_recv()
                    value = value + y_in[n].astype(F32)
                for c in range(2):
                    part = value[:, c * 128 : (c + 1) * 128]
                    m_own[3 * c + b, half(h)] = part
                    m_out[3 * c + b, half(h)] = part.astype(BF16)
            for c in range(2):
                n = 3 * c + b

                @pl.when(z != n)
                def _():
                    pltpu.make_async_remote_copy(
                        src_ref=m_out.at[n], dst_ref=m_in.at[z], send_sem=m_send.at[n], recv_sem=m_recv.at[z],
                        device_id=(o, y * NZ + n), device_id_type=MESH,
                    ).start()
            return
        if t % 2 == 1:
            product(b, p_up, yp(d))
            product(b, p_down, yp(-d))
            hop(b, 0, 1, p_up)
            hop(b, 1, 0, p_down)
        else:
            hop(b, 0, 0, p_up)
            hop(b, 1, 1, p_down)

    far_1(0)
    terms(term, core)
    far_2(0)
    far_1(1)
    far_3(0)
    far_2(1)
    far_1(2)
    grad_1()
    far_3(1)
    far_4(0)
    tick(0, 0)
    tick(0, 1)
    far_2(2)
    tick(0, 2)
    far_3(2)
    grad_2()
    far_4(1)
    tick(1, 0)
    tick(0, 3)
    tick(1, 1)
    tick(0, 4)
    far_4(2)
    tick(1, 2)
    tick(2, 0)
    tick(0, 5)
    tick(1, 3)
    tick(2, 1)
    grad_3()
    tick(0, 6)
    tick(1, 4)
    tick(2, 2)
    tick(0, 7)
    tick(1, 5)
    tick(2, 3)
    tick(1, 6)
    tick(2, 4)
    tick(1, 7)
    tick(2, 5)
    tick(2, 6)
    tick(2, 7)

    acc[...] = jnp.zeros_like(acc)

    def act_block(k, carry):
        total = acc[...]
        for b in range(NS):
            g = jnp.concatenate([scaled[k, 0, b], scaled[k, 1, b]], axis=1)
            w = jnp.concatenate([weight[k, 0, b], weight[k, 1, b]], axis=1)
            total += lax.dot_general(g, w, (((1,), (1,)), ((), ())), preferred_element_type=F32)
        acc[...] = total
        return carry

    lax.fori_loop(0, NY, act_block, 0)
    act_grad_ref[...] = acc[...].astype(BF16)

    b_z[0].wait_recv()
    wgrad_ref[...] += z_in[...].astype(F32)

    acc[:, :128] = m_own[z]
    for n in range(NZ):

        @pl.when(z != n)
        def _():
            copy = pltpu.make_async_remote_copy(
                src_ref=m_out.at[n], dst_ref=m_in.at[n], send_sem=m_send.at[n], recv_sem=m_recv.at[n],
                device_id=(o, y * NZ + n), device_id_type=MESH,
            )
            copy.wait_recv()
            acc[:, :128] += m_in[n].astype(F32)
            copy.wait_send()

    mixed_ref[...] = (coef[...] * acc[:, :128]).astype(BF16)
    for copy in sent:
        copy.wait_send()


def local(acts, codes, scales, routes, route_logits, cotangent):
    vmem = pl.BlockSpec(memory_space=pltpu.VMEM)
    dma = pltpu.SemaphoreType.DMA
    blk = (FFD, COLS)
    return tuple(
        pl.pallas_call(
            kernel,
            name="expert_down",
            out_shape=(
                jax.ShapeDtypeStruct((TOK, 128), BF16),
                jax.ShapeDtypeStruct((TOK, FFD), BF16),
                jax.ShapeDtypeStruct(blk, F32),
            ),
            in_specs=[pl.BlockSpec(memory_space=pltpu.HBM)] * 6,
            out_specs=[vmem] * 3,
            scratch_shapes=[
                pltpu.VMEM((TOK, FFD), BF16),
                pltpu.VMEM(blk, BF16),
                pltpu.VMEM((8, FFD), F32),
                pltpu.VMEM((2, TOK), jnp.int32),
                pltpu.VMEM((2, TOK), F32),
                pltpu.VMEM((TOK, 16 * COLS), BF16),
                pltpu.VMEM((NY, 2, NS, FFD, 128), BF16),
                pltpu.VMEM((NY, 2, NS, TOK, 128), BF16),
                pltpu.VMEM((TOK, 1), F32),
                pltpu.VMEM((FFD, TOK), BF16),
                pltpu.VMEM((NY, *blk), BF16),
                pltpu.VMEM((NY, *blk), BF16),
                pltpu.VMEM((NY, *blk), BF16),
                pltpu.VMEM((2, 2, HALF, COLS), BF16),
                pltpu.VMEM((2, 2, HALF, COLS), BF16),
                pltpu.VMEM((2, 2, *blk), BF16),
                pltpu.VMEM((2, 2, *blk), BF16),
                pltpu.VMEM(blk, BF16),
                pltpu.VMEM(blk, BF16),
                pltpu.VMEM((2 * NS, TOK, 256), F32),
                pltpu.VMEM((N_HOP, HALF, 256), BF16),
                pltpu.VMEM((N_HOP, HALF, 256), BF16),
                pltpu.VMEM((NZ, TOK, 128), F32),
                pltpu.VMEM((NZ, TOK, 128), BF16),
                pltpu.VMEM((NZ, TOK, 128), BF16),
                pltpu.VMEM((TOK, FFD), F32),
                dma((6,)), dma((N_COPY,)), dma((N_COPY,)), dma((NZ,)), dma((NZ,)),
            ],
            compiler_params=pltpu.CompilerParams(
                collective_id=0, has_side_effects=True, vmem_limit_bytes=36 * 2**20
            ),
            cost_estimate=pl.CostEstimate(flops=2_500_000_000, bytes_accessed=8_000_000, transcendentals=0),
        )(*(pltpu.with_memory_space_constraint(a, pltpu.HBM) for a in (acts, codes, scales, routes.T, route_logits.T, cotangent)))
    )


def solution(mesh):
    in_specs = (
        P("outer", "inner"),
        P("inner", "outer"),
        P("outer", "inner"),
        P("outer", None),
        P("outer", None),
        P("outer", None),
    )
    out_specs = (P("outer", "inner"), P("outer", "inner"), P("inner", "outer"))
    return jax.shard_map(local, mesh=mesh, in_specs=in_specs, out_specs=out_specs, check_vma=False)
```

```python
import jax
import jax.numpy as jnp
from jax import lax
from jax.experimental import pallas as pl
from jax.experimental.pallas import tpu as pltpu
from jax.sharding import PartitionSpec as P

MESH = pl.DeviceIdType.MESH
BF16 = jnp.bfloat16
F32 = jnp.float32
NX, NY, NZ = 4, 8, 6
TOK, FFD, COLS = 256, 256, 384
HALF = FFD // 2
NS = 3
N_HOP, N_COPY = 14 * NS, 88


def kernel(
    acts_ref, codes_ref, scales_ref, routes_ref, logits_ref, cot_ref,
    mixed_ref, act_grad_ref, wgrad_ref,
    acts_v, codes_v, scales_v, routes_v, logits_v, cot_v,
    weight, scaled, coef, acts_t, term_out, term_in, term,
    x1_out, x1_in, x2_out, x2_in, z_out, z_in,
    prod, y_out, y_in, m_own, m_out, m_in, acc,
    in_sem, s_sem, r_sem, m_send, m_recv,
):
    o = lax.axis_index("outer")
    i = lax.axis_index("inner")
    core = lax.rem(o, 2)
    chip = lax.div(o, 2)
    x = lax.rem(chip, NX)
    hi = lax.div(chip, NX)
    y = lax.div(i, NZ)
    z = lax.rem(i, NZ)

    def xp(n):
        return lax.rem(x + n + NX, NX)

    def yp(n):
        return lax.rem(y + n + NY, NY)

    sibling = (chip * 2 + 1 - core, i)
    partner = (((1 - hi) * NX + x) * 2 + core, i)
    right, left = ((hi * NX + xp(1)) * 2 + core, i), ((hi * NX + xp(-1)) * 2 + core, i)
    across = ((hi * NX + xp(2)) * 2 + core, i)
    up, down = (o, yp(1) * NZ + z), (o, yp(-1) * NZ + z)

    def load(n, src, dst):
        copy = pltpu.make_async_copy(src, dst, in_sem.at[n])
        copy.start()
        return copy

    scales_v[...] = jnp.zeros_like(scales_v)
    loads = [
        load(0, scales_ref, scales_v.at[pl.ds(0, 3)]),
        load(1, codes_ref, codes_v),
        load(2, routes_ref, routes_v),
        load(3, logits_ref, logits_v),
        load(4, acts_ref, acts_v),
        load(5, cot_ref, cot_v),
    ]

    barrier = pltpu.get_barrier_semaphore()
    for peer in (sibling, partner, right, left, across, up, down):
        pl.semaphore_signal(barrier, inc=1, device_id=peer, device_id_type=MESH)
    for n in range(1, NZ):
        pl.semaphore_signal(barrier, inc=1, device_id=(o, y * NZ + lax.rem(z + n, NZ)), device_id_type=MESH)

    loads[0].wait()
    factors = scales_v[...].T
    loads[1].wait()
    for b in range(NS):
        cols = pl.ds(b * 128, 128)
        weight[chip, core, b] = (codes_v[:, cols].astype(F32) * factors[:, b : b + 1]).astype(BF16)
    pl.semaphore_wait(barrier, 7 + NZ - 1)

    sent = []

    def send(src, dst, peer):
        n = len(sent)
        copy = pltpu.make_async_remote_copy(
            src_ref=src, dst_ref=dst, send_sem=s_sem.at[n], recv_sem=r_sem.at[n],
            device_id=peer, device_id_type=MESH,
        )
        copy.start()
        sent.append(copy)
        return copy

    def same(ref, peer):
        return send(ref, ref, peer)

    far = 1 - hi
    far_z = [same(weight.at[chip, core, b], partner) for b in range(NS)]
    own = weight.at[chip, core]
    own_x = [same(own, peer) for peer in (right, left, across)]
    own_shared = [same(own, sibling)]

    loads[2].wait()
    loads[3].wait()
    lg = logits_v[...]
    ex = jnp.exp(lg - jnp.max(lg, axis=0, keepdims=True))
    probs = ex / jnp.sum(ex, axis=0, keepdims=True)
    row = jnp.sum(probs * (routes_v[...] == 0).astype(F32), axis=0, keepdims=True)
    coef[...] = jnp.broadcast_to(row, (8, TOK)).T[:, :1]
    loads[4].wait()
    acts_t[...] = acts_v[...].T
    loads[5].wait()

    def scale_chip(k, carry):
        for c in range(2):
            for b in range(NS):
                cols = pl.ds(pl.multiple_of(k * (2 * COLS), 128) + (c * COLS + b * 128), 128)
                scaled[k, c, b] = (coef[...] * cot_v[:, cols].astype(F32)).astype(BF16)
        return carry

    lax.fori_loop(0, NY, scale_chip, 0)

    def own_near():
        for copy, n in zip(own_x, (-1, 1, 2)):
            copy.wait_recv()
            own_shared.append(same(weight.at[hi * NX + xp(n), core], sibling))

    own_near()

    def terms(dst, c):
        def body(k, carry):
            g = jnp.concatenate([scaled[k, c, b] for b in range(NS)], axis=1)
            dst[k] = jnp.dot(acts_t[...], g, preferred_element_type=F32).astype(BF16)
            return carry

        lax.fori_loop(0, NY, body, 0)

    terms(term_out, 1 - core)
    b_pair = send(term_out, term_in, sibling)

    far_x, far_shared = [None] * NS, [[] for _ in range(NS)]

    def far_1(b):
        far_z[b].wait_recv()
        w = weight.at[far * NX + x, core, b]
        far_x[b] = [same(w, peer) for peer in (right, left, across)]
        far_shared[b].append(same(w, sibling))

    def far_2(b):
        for copy, n in zip(far_x[b], (-1, 1, 2)):
            copy.wait_recv()
            far_shared[b].append(same(weight.at[far * NX + xp(n), core, b], sibling))

    def far_4(b):
        if b == 0:
            for copy in own_shared:
                copy.wait_recv()
        for copy in far_shared[b]:
            copy.wait_recv()

    b_x1, b_x2, b_z = [], [], []

    def paired(n, rows):
        return term[n, rows].astype(F32) + term_in[n, rows].astype(F32)

    def half(d):
        return pl.ds(d * HALF, HALF)

    def grad_1():
        b_pair.wait_recv()
        for w in (far, hi):
            for d in range(2):
                x1_out[d, w] = paired(w * NX + xp(2), half(d)).astype(BF16)
                b_x1.append(send(x1_out.at[d, w], x1_in.at[d, w], (right, left)[d]))

    def grad_2():
        for d in range(2):
            for w in range(2):
                n = w * NX + xp(1 - 2 * d)
                x2_out[d, w, half(1 - d)] = paired(n, half(1 - d)).astype(BF16)
        for k in range(2):
            w = (far, hi)[k]
            for d in range(2):
                b_x1[2 * k + d].wait_recv()
                n = w * NX + xp(1 - 2 * d)
                x2_out[d, w, half(d)] = (paired(n, half(d)) + x1_in[d, w].astype(F32)).astype(BF16)
                b_x2.append(send(x2_out.at[d, w], x2_in.at[d, w], (right, left)[d]))

    def reduced(w):
        return paired(w * NX + x, pl.ds(0, FFD)) + x2_in[0, w].astype(F32) + x2_in[1, w].astype(F32)

    def grad_3():
        for copy in b_x2[:2]:
            copy.wait_recv()
        z_out[...] = reduced(far).astype(BF16)
        b_z.append(send(z_out, z_in, partner))

    def grad_4():
        for copy in b_x2[2:]:
            copy.wait_recv()
        wgrad_ref[...] = reduced(hi)

    chains = [{} for _ in range(NS)]

    def product(b, slot, dest):
        w = jnp.concatenate([weight[dest, 0, b], weight[dest, 1, b]], axis=1)
        prod[slot] = jnp.dot(acts_v[...], w, preferred_element_type=F32)

    def hop(b, way, h, slot):
        prior = chains[b].get((way, h))
        value = prod[slot, half(h)]
        if prior is not None:
            n, copy = prior
            copy.wait_recv()
            value = value + y_in[n].astype(F32)
        n = hop.count
        hop.count += 1
        y_out[n] = value.astype(BF16)
        chains[b][(way, h)] = n, send(y_out.at[n], y_in.at[n], (up, down)[way])

    hop.count = 0

    def tick(b, t):
        p_up, p_down = 2 * b, 2 * b + 1
        if t == 0:
            product(b, p_up, yp(4))
            hop(b, 0, 0, p_up)
            hop(b, 1, 1, p_up)
            return
        d = 3 - (t - 1) // 2
        if t == 7:
            product(b, p_up, y)
            for h in range(2):
                value = prod[p_up, half(h)]
                for way in range(2):
                    n, copy = chains[b][(way, h)]
                    copy.wait_recv()
                    value = value + y_in[n].astype(F32)
                for c in range(2):
                    part = value[:, c * 128 : (c + 1) * 128]
                    m_own[3 * c + b, half(h)] = part
                    m_out[3 * c + b, half(h)] = part.astype(BF16)
            for c in range(2):
                n = 3 * c + b

                @pl.when(z != n)
                def _():
                    pltpu.make_async_remote_copy(
                        src_ref=m_out.at[n], dst_ref=m_in.at[z], send_sem=m_send.at[n], recv_sem=m_recv.at[z],
                        device_id=(o, y * NZ + n), device_id_type=MESH,
                    ).start()
            return
        if t % 2 == 1:
            product(b, p_up, yp(d))
            product(b, p_down, yp(-d))
            hop(b, 0, 1, p_up)
            hop(b, 1, 0, p_down)
        else:
            hop(b, 0, 0, p_up)
            hop(b, 1, 1, p_down)

    def act_block(k):
        total = acc[...] if k else None
        for b in range(NS):
            g = jnp.concatenate([scaled[k, 0, b], scaled[k, 1, b]], axis=1)
            w = jnp.concatenate([weight[k, 0, b], weight[k, 1, b]], axis=1)
            part = lax.dot_general(g, w, (((1,), (1,)), ((), ())), preferred_element_type=F32)
            total = part if total is None else total + part
        if k < NY - 1:
            acc[...] = total
        else:
            act_grad_ref[...] = total.astype(BF16)

    far_1(0)
    terms(term, core)
    far_1(1)
    far_2(0)
    far_1(2)
    far_2(1)
    far_4(0)
    grad_1()
    tick(0, 0)
    tick(0, 1)
    far_2(2)
    far_4(1)
    tick(0, 2)
    tick(1, 0)
    grad_2()
    tick(0, 3)
    tick(1, 1)
    far_4(2)
    tick(0, 4)
    tick(1, 2)
    tick(2, 0)
    tick(0, 5)
    tick(1, 3)
    tick(2, 1)
    grad_3()
    tick(0, 6)
    tick(1, 4)
    tick(2, 2)
    tick(0, 7)
    tick(1, 5)
    act_block(0)
    tick(2, 3)
    act_block(1)
    tick(1, 6)
    act_block(2)
    tick(2, 4)
    act_block(3)
    tick(1, 7)
    act_block(4)
    tick(2, 5)
    act_block(5)
    tick(2, 6)
    act_block(6)
    tick(2, 7)
    act_block(7)

    grad_4()
    b_z[0].wait_recv()
    wgrad_ref[...] += z_in[...].astype(F32)

    acc[:, :128] = m_own[z]
    for n in range(NZ):

        @pl.when(z != n)
        def _():
            copy = pltpu.make_async_remote_copy(
                src_ref=m_out.at[n], dst_ref=m_in.at[n], send_sem=m_send.at[n], recv_sem=m_recv.at[n],
                device_id=(o, y * NZ + n), device_id_type=MESH,
            )
            copy.wait_recv()
            acc[:, :128] += m_in[n].astype(F32)
            copy.wait_send()

    mixed_ref[...] = (coef[...] * acc[:, :128]).astype(BF16)
    for copy in sent:
        copy.wait_send()


def local(acts, codes, scales, routes, route_logits, cotangent):
    vmem = pl.BlockSpec(memory_space=pltpu.VMEM)
    dma = pltpu.SemaphoreType.DMA
    blk = (FFD, COLS)
    return tuple(
        pl.pallas_call(
            kernel,
            name="expert_down",
            out_shape=(
                jax.ShapeDtypeStruct((TOK, 128), BF16),
                jax.ShapeDtypeStruct((TOK, FFD), BF16),
                jax.ShapeDtypeStruct(blk, F32),
            ),
            in_specs=[pl.BlockSpec(memory_space=pltpu.HBM)] * 6,
            out_specs=[vmem] * 3,
            scratch_shapes=[
                pltpu.VMEM((TOK, FFD), BF16),
                pltpu.VMEM(blk, BF16),
                pltpu.VMEM((8, FFD), F32),
                pltpu.VMEM((2, TOK), jnp.int32),
                pltpu.VMEM((2, TOK), F32),
                pltpu.VMEM((TOK, 16 * COLS), BF16),
                pltpu.VMEM((NY, 2, NS, FFD, 128), BF16),
                pltpu.VMEM((NY, 2, NS, TOK, 128), BF16),
                pltpu.VMEM((TOK, 1), F32),
                pltpu.VMEM((FFD, TOK), BF16),
                pltpu.VMEM((NY, *blk), BF16),
                pltpu.VMEM((NY, *blk), BF16),
                pltpu.VMEM((NY, *blk), BF16),
                pltpu.VMEM((2, 2, HALF, COLS), BF16),
                pltpu.VMEM((2, 2, HALF, COLS), BF16),
                pltpu.VMEM((2, 2, *blk), BF16),
                pltpu.VMEM((2, 2, *blk), BF16),
                pltpu.VMEM(blk, BF16),
                pltpu.VMEM(blk, BF16),
                pltpu.VMEM((2 * NS, TOK, 256), F32),
                pltpu.VMEM((N_HOP, HALF, 256), BF16),
                pltpu.VMEM((N_HOP, HALF, 256), BF16),
                pltpu.VMEM((NZ, TOK, 128), F32),
                pltpu.VMEM((NZ, TOK, 128), BF16),
                pltpu.VMEM((NZ, TOK, 128), BF16),
                pltpu.VMEM((TOK, FFD), F32),
                dma((6,)), dma((N_COPY,)), dma((N_COPY,)), dma((NZ,)), dma((NZ,)),
            ],
            compiler_params=pltpu.CompilerParams(
                collective_id=0, has_side_effects=True, vmem_limit_bytes=36 * 2**20
            ),
            cost_estimate=pl.CostEstimate(flops=2_500_000_000, bytes_accessed=8_000_000, transcendentals=0),
        )(*(pltpu.with_memory_space_constraint(a, pltpu.HBM) for a in (acts, codes, scales, routes.T, route_logits.T, cotangent)))
    )


def solution(mesh):
    in_specs = (
        P("outer", "inner"),
        P("inner", "outer"),
        P("outer", "inner"),
        P("outer", None),
        P("outer", None),
        P("outer", None),
    )
    out_specs = (P("outer", "inner"), P("outer", "inner"), P("inner", "outer"))
    return jax.shard_map(local, mesh=mesh, in_specs=in_specs, out_specs=out_specs, check_vma=False)
```

```python
import jax
import jax.numpy as jnp
from jax import lax
from jax.experimental import pallas as pl
from jax.experimental.pallas import tpu as pltpu
from jax.sharding import PartitionSpec as P

MESH = pl.DeviceIdType.MESH
BF16 = jnp.bfloat16
F32 = jnp.float32
NX, NY, NZ = 4, 8, 6
TOK, FFD, COLS = 256, 256, 384
HALF = FFD // 2
NS = 3
N_HOP, N_COPY = 14 * NS, 88


def kernel(
    acts_ref, codes_ref, scales_ref, routes_ref, logits_ref, cot_ref,
    mixed_ref, act_grad_ref, wgrad_ref,
    acts_v, codes_v, scales_v, routes_v, logits_v, cot_v,
    weight, scaled, coef, acts_t, term_out, term_in, term,
    x1_out, x1_in, x2_out, x2_in, z_out, z_in,
    prod, y_out, y_in, m_own, m_out, m_in, acc,
    in_sem, s_sem, r_sem, m_send, m_recv,
):
    o = lax.axis_index("outer")
    i = lax.axis_index("inner")
    core = lax.rem(o, 2)
    chip = lax.div(o, 2)
    x = lax.rem(chip, NX)
    hi = lax.div(chip, NX)
    y = lax.div(i, NZ)
    z = lax.rem(i, NZ)

    def xp(n):
        return lax.rem(x + n + NX, NX)

    def yp(n):
        return lax.rem(y + n + NY, NY)

    sibling = (chip * 2 + 1 - core, i)
    partner = (((1 - hi) * NX + x) * 2 + core, i)
    right, left = ((hi * NX + xp(1)) * 2 + core, i), ((hi * NX + xp(-1)) * 2 + core, i)
    across = ((hi * NX + xp(2)) * 2 + core, i)
    up, down = (o, yp(1) * NZ + z), (o, yp(-1) * NZ + z)

    def load(n, src, dst):
        copy = pltpu.make_async_copy(src, dst, in_sem.at[n])
        copy.start()
        return copy

    scales_v[...] = jnp.zeros_like(scales_v)
    loads = [
        load(0, scales_ref, scales_v.at[pl.ds(0, 3)]),
        load(1, codes_ref, codes_v),
        load(2, routes_ref, routes_v),
        load(3, logits_ref, logits_v),
        load(4, acts_ref, acts_v),
        load(5, cot_ref, cot_v),
    ]

    barrier = pltpu.get_barrier_semaphore()
    for peer in (sibling, partner, right, left, across, up, down):
        pl.semaphore_signal(barrier, inc=1, device_id=peer, device_id_type=MESH)
    for n in range(1, NZ):
        pl.semaphore_signal(barrier, inc=1, device_id=(o, y * NZ + lax.rem(z + n, NZ)), device_id_type=MESH)

    loads[0].wait()
    factors = scales_v[...].T
    loads[1].wait()
    for b in range(NS):
        cols = pl.ds(b * 128, 128)
        weight[chip, core, b] = (codes_v[:, cols].astype(F32) * factors[:, b : b + 1]).astype(BF16)
    pl.semaphore_wait(barrier, 7 + NZ - 1)

    sent = []

    def send(src, dst, peer):
        n = len(sent)
        copy = pltpu.make_async_remote_copy(
            src_ref=src, dst_ref=dst, send_sem=s_sem.at[n], recv_sem=r_sem.at[n],
            device_id=peer, device_id_type=MESH,
        )
        copy.start()
        sent.append(copy)
        return copy

    def same(ref, peer):
        return send(ref, ref, peer)

    far = 1 - hi
    far_z = [same(weight.at[chip, core, b], partner) for b in range(NS)]
    own = weight.at[chip, core]
    own_x = [same(own, peer) for peer in (across, right, left)]
    own_shared = [same(own, sibling)]

    loads[2].wait()
    loads[3].wait()
    lg = logits_v[...]
    ex = jnp.exp(lg - jnp.max(lg, axis=0, keepdims=True))
    probs = ex / jnp.sum(ex, axis=0, keepdims=True)
    row = jnp.sum(probs * (routes_v[...] == 0).astype(F32), axis=0, keepdims=True)
    coef[...] = jnp.broadcast_to(row, (8, TOK)).T[:, :1]
    loads[4].wait()
    acts_t[...] = acts_v[...].T
    loads[5].wait()

    def scale_chip(k, carry):
        for c in range(2):
            for b in range(NS):
                cols = pl.ds(pl.multiple_of(k * (2 * COLS), 128) + (c * COLS + b * 128), 128)
                scaled[k, c, b] = (coef[...] * cot_v[:, cols].astype(F32)).astype(BF16)
        return carry

    lax.fori_loop(0, NY, scale_chip, 0)

    def own_near():
        for copy, n in zip(own_x[1:] + own_x[:1], (-1, 1, 2)):
            copy.wait_recv()
            own_shared.append(same(weight.at[hi * NX + xp(n), core], sibling))

    own_near()

    def terms(dst, c):
        def body(k, carry):
            g = jnp.concatenate([scaled[k, c, b] for b in range(NS)], axis=1)
            dst[k] = jnp.dot(acts_t[...], g, preferred_element_type=F32).astype(BF16)
            return carry

        lax.fori_loop(0, NY, body, 0)

    terms(term_out, 1 - core)
    b_pair = send(term_out, term_in, sibling)

    far_x, far_shared = [None] * NS, [[] for _ in range(NS)]

    def far_1(b):
        far_z[b].wait_recv()
        w = weight.at[far * NX + x, core, b]
        far_x[b] = [same(w, peer) for peer in (across, right, left)]
        far_shared[b].append(same(w, sibling))

    def far_2(b):
        for copy, n in zip(far_x[b][1:] + far_x[b][:1], (-1, 1, 2)):
            copy.wait_recv()
            far_shared[b].append(same(weight.at[far * NX + xp(n), core, b], sibling))

    def far_4(b):
        if b == 0:
            for copy in own_shared:
                copy.wait_recv()
        for copy in far_shared[b]:
            copy.wait_recv()

    b_x1, b_x2, b_z = [], [], []

    def paired(n, rows):
        return term[n, rows].astype(F32) + term_in[n, rows].astype(F32)

    def half(d):
        return pl.ds(d * HALF, HALF)

    def grad_1():
        b_pair.wait_recv()
        for w in (far, hi):
            for d in range(2):
                x1_out[d, w] = paired(w * NX + xp(2), half(d)).astype(BF16)
                b_x1.append(send(x1_out.at[d, w], x1_in.at[d, w], (right, left)[d]))

    def grad_2():
        for d in range(2):
            for w in range(2):
                n = w * NX + xp(1 - 2 * d)
                x2_out[d, w, half(1 - d)] = paired(n, half(1 - d)).astype(BF16)
        for k in range(2):
            w = (far, hi)[k]
            for d in range(2):
                b_x1[2 * k + d].wait_recv()
                n = w * NX + xp(1 - 2 * d)
                x2_out[d, w, half(d)] = (paired(n, half(d)) + x1_in[d, w].astype(F32)).astype(BF16)
                b_x2.append(send(x2_out.at[d, w], x2_in.at[d, w], (right, left)[d]))

    def reduced(w):
        return paired(w * NX + x, pl.ds(0, FFD)) + x2_in[0, w].astype(F32) + x2_in[1, w].astype(F32)

    def grad_3():
        for copy in b_x2[:2]:
            copy.wait_recv()
        z_out[...] = reduced(far).astype(BF16)
        b_z.append(send(z_out, z_in, partner))

    def grad_4():
        for copy in b_x2[2:]:
            copy.wait_recv()
        wgrad_ref[...] = reduced(hi)

    chains = [{} for _ in range(NS)]

    def product(b, slot, dest):
        w = jnp.concatenate([weight[dest, 0, b], weight[dest, 1, b]], axis=1)
        prod[slot] = jnp.dot(acts_v[...], w, preferred_element_type=F32)

    def hop(b, way, h, slot):
        prior = chains[b].get((way, h))
        value = prod[slot, half(h)]
        if prior is not None:
            n, copy = prior
            copy.wait_recv()
            value = value + y_in[n].astype(F32)
        n = hop.count
        hop.count += 1
        y_out[n] = value.astype(BF16)
        chains[b][(way, h)] = n, send(y_out.at[n], y_in.at[n], (up, down)[way])

    hop.count = 0

    def tick(b, t):
        p_up, p_down = 2 * b, 2 * b + 1
        if t == 0:
            product(b, p_up, yp(4))
            hop(b, 0, 0, p_up)
            hop(b, 1, 1, p_up)
            return
        d = 3 - (t - 1) // 2
        if t == 7:
            product(b, p_up, y)
            for h in range(2):
                value = prod[p_up, half(h)]
                for way in range(2):
                    n, copy = chains[b][(way, h)]
                    copy.wait_recv()
                    value = value + y_in[n].astype(F32)
                for c in range(2):
                    part = value[:, c * 128 : (c + 1) * 128]
                    m_own[3 * c + b, half(h)] = part
                    m_out[3 * c + b, half(h)] = part.astype(BF16)
            for c in range(2):
                n = 3 * c + b

                @pl.when(z != n)
                def _():
                    pltpu.make_async_remote_copy(
                        src_ref=m_out.at[n], dst_ref=m_in.at[z], send_sem=m_send.at[n], recv_sem=m_recv.at[z],
                        device_id=(o, y * NZ + n), device_id_type=MESH,
                    ).start()
            return
        if t % 2 == 1:
            product(b, p_up, yp(d))
            product(b, p_down, yp(-d))
            hop(b, 0, 1, p_up)
            hop(b, 1, 0, p_down)
        else:
            hop(b, 0, 0, p_up)
            hop(b, 1, 1, p_down)

    def act_block(k):
        total = acc[...] if k else None
        for b in range(NS):
            g = jnp.concatenate([scaled[k, 0, b], scaled[k, 1, b]], axis=1)
            w = jnp.concatenate([weight[k, 0, b], weight[k, 1, b]], axis=1)
            part = lax.dot_general(g, w, (((1,), (1,)), ((), ())), preferred_element_type=F32)
            total = part if total is None else total + part
        if k < NY - 1:
            acc[...] = total
        else:
            act_grad_ref[...] = total.astype(BF16)

    far_1(0)
    terms(term, core)
    far_1(1)
    far_2(0)
    far_1(2)
    far_2(1)
    far_4(0)
    grad_1()
    tick(0, 0)
    tick(0, 1)
    far_2(2)
    far_4(1)
    tick(0, 2)
    tick(1, 0)
    grad_2()
    tick(0, 3)
    tick(1, 1)
    far_4(2)
    tick(0, 4)
    tick(1, 2)
    tick(2, 0)
    tick(0, 5)
    tick(1, 3)
    tick(2, 1)
    grad_3()
    tick(0, 6)
    tick(1, 4)
    tick(2, 2)
    tick(0, 7)
    tick(1, 5)
    act_block(0)
    tick(2, 3)
    act_block(1)
    tick(1, 6)
    act_block(2)
    tick(2, 4)
    act_block(3)
    tick(1, 7)
    act_block(4)
    tick(2, 5)
    act_block(5)
    tick(2, 6)
    act_block(6)
    tick(2, 7)
    act_block(7)

    grad_4()
    b_z[0].wait_recv()
    wgrad_ref[...] += z_in[...].astype(F32)

    acc[:, :128] = m_own[z]
    for n in range(NZ):

        @pl.when(z != n)
        def _():
            copy = pltpu.make_async_remote_copy(
                src_ref=m_out.at[n], dst_ref=m_in.at[n], send_sem=m_send.at[n], recv_sem=m_recv.at[n],
                device_id=(o, y * NZ + n), device_id_type=MESH,
            )
            copy.wait_recv()
            acc[:, :128] += m_in[n].astype(F32)
            copy.wait_send()

    mixed_ref[...] = (coef[...] * acc[:, :128]).astype(BF16)
    for copy in sent:
        copy.wait_send()


def local(acts, codes, scales, routes, route_logits, cotangent):
    vmem = pl.BlockSpec(memory_space=pltpu.VMEM)
    dma = pltpu.SemaphoreType.DMA
    blk = (FFD, COLS)
    return tuple(
        pl.pallas_call(
            kernel,
            name="expert_down",
            out_shape=(
                jax.ShapeDtypeStruct((TOK, 128), BF16),
                jax.ShapeDtypeStruct((TOK, FFD), BF16),
                jax.ShapeDtypeStruct(blk, F32),
            ),
            in_specs=[pl.BlockSpec(memory_space=pltpu.HBM)] * 6,
            out_specs=[vmem] * 3,
            scratch_shapes=[
                pltpu.VMEM((TOK, FFD), BF16),
                pltpu.VMEM(blk, BF16),
                pltpu.VMEM((8, FFD), F32),
                pltpu.VMEM((2, TOK), jnp.int32),
                pltpu.VMEM((2, TOK), F32),
                pltpu.VMEM((TOK, 16 * COLS), BF16),
                pltpu.VMEM((NY, 2, NS, FFD, 128), BF16),
                pltpu.VMEM((NY, 2, NS, TOK, 128), BF16),
                pltpu.VMEM((TOK, 1), F32),
                pltpu.VMEM((FFD, TOK), BF16),
                pltpu.VMEM((NY, *blk), BF16),
                pltpu.VMEM((NY, *blk), BF16),
                pltpu.VMEM((NY, *blk), BF16),
                pltpu.VMEM((2, 2, HALF, COLS), BF16),
                pltpu.VMEM((2, 2, HALF, COLS), BF16),
                pltpu.VMEM((2, 2, *blk), BF16),
                pltpu.VMEM((2, 2, *blk), BF16),
                pltpu.VMEM(blk, BF16),
                pltpu.VMEM(blk, BF16),
                pltpu.VMEM((2 * NS, TOK, 256), F32),
                pltpu.VMEM((N_HOP, HALF, 256), BF16),
                pltpu.VMEM((N_HOP, HALF, 256), BF16),
                pltpu.VMEM((NZ, TOK, 128), F32),
                pltpu.VMEM((NZ, TOK, 128), BF16),
                pltpu.VMEM((NZ, TOK, 128), BF16),
                pltpu.VMEM((TOK, FFD), F32),
                dma((6,)), dma((N_COPY,)), dma((N_COPY,)), dma((NZ,)), dma((NZ,)),
            ],
            compiler_params=pltpu.CompilerParams(
                collective_id=0, has_side_effects=True, vmem_limit_bytes=36 * 2**20
            ),
            cost_estimate=pl.CostEstimate(flops=2_500_000_000, bytes_accessed=8_000_000, transcendentals=0),
        )(*(pltpu.with_memory_space_constraint(a, pltpu.HBM) for a in (acts, codes, scales, routes.T, route_logits.T, cotangent)))
    )


def solution(mesh):
    in_specs = (
        P("outer", "inner"),
        P("inner", "outer"),
        P("outer", "inner"),
        P("outer", None),
        P("outer", None),
        P("outer", None),
    )
    out_specs = (P("outer", "inner"), P("outer", "inner"), P("inner", "outer"))
    return jax.shard_map(local, mesh=mesh, in_specs=in_specs, out_specs=out_specs, check_vma=False)
```
